768 devices in a mesh: row: 12 (over z_hi, x), col: 64 (over y, z_lo, core).
Axes of the slice: x: 4, y: 8, z: 12 (z_hi: 3, z_lo: 4; z = z_hi * 4 + z_lo), core: 2. Of those that a mesh axis runs over, the one named last changes fastest.
Arguments:
- gate_pre: bfloat16 [1536, 26624], P('row', 'col'), may hold values from -16 to 16
- up_pre: bfloat16 [1536, 26624], P('row', 'col'), may hold values from -6 to 6
- down_weight: bfloat16 [26624, 9216], P('col', 'row'), may hold values from -0.0390625 to 0.0390625
- out_grad: bfloat16 [1536, 9216], P('col', 'row'), may hold values from -6 to 6
- noised: int32 [1536], P('col'), may hold values from 0 to 1, as said below
Outputs:
- layer_out: bfloat16 [1536, 9216], P('col', 'row')
- gate_grad: bfloat16 [1536, 26624], P('row', 'col')
- up_grad: bfloat16 [1536, 26624], P('row', 'col')
- weight_grad: bfloat16 [26624, 9216], P('col', 'row')
The draws below stay inside these ranges and needn't reach their ends.
Inputs may be any that keep to these rules, and one draw needn't show every extreme that they name: Every aligned block of 24 tokens holds at least one noised token.
All inputs are finite; a program needn't handle non-finite values.
Results may differ from the reference program's by a relative error of at most 0.018.
Values may be sent and summed in bfloat16 or wider, within the bound.
A program may use at most 32 MiB of HBM per device.

```python
import jax
import jax.numpy as jnp

D = 9216
FF = 26624
TOKENS = 1536
TOK_COL = 24
N_ROW = 12


def draw_noised(key, part):
    key = jax.random.fold_in(key, 7)
    first, second = jax.random.split(key)
    place = jnp.arange(TOKENS, dtype=jnp.int32)
    limit = 200 + 600 * place // TOKENS
    picks = jax.random.randint(first, (TOKENS,), 0, 1000, dtype=jnp.int32)
    flags = (picks < limit).astype(jnp.int32)
    chosen = jax.random.randint(second, (TOKENS // TOK_COL,), 0, TOK_COL, dtype=jnp.int32)
    forced = (place % TOK_COL == jnp.repeat(chosen, TOK_COL)).astype(jnp.int32)
    return jnp.maximum(flags, forced)


def raised(values, rng, source, target, shards_of, factor):
    def block_of(dim):
        return (jnp.arange(values.shape[dim]) // (values.shape[dim] // shards_of)).reshape((-1,) + (1,) * (values.ndim - 1 - dim))

    near = jax.random.permutation(rng, shards_of)[block_of(target)]
    second = (block_of(target) + shards_of // 2) % shards_of
    return jnp.where((block_of(source) == near) | (block_of(source) == second), factor * values, values)


def shard_levels(key, dims, cuts, low, high):
    def one(position, blocks):
        steps = jax.random.uniform(jax.random.fold_in(jax.random.fold_in(key, 6), position), (blocks,), jnp.float32, low / len(cuts), high / len(cuts))
        return jnp.repeat(jnp.exp(steps), dims[position] // blocks).reshape((-1,) + (1,) * (len(dims) - position - 1))

    gain = one(*cuts[0])
    for cut in cuts[1:]:
        gain = gain * one(*cut)
    return gain


def scatter_about(rng, extent, scale, most, pieces=(), kind=jnp.bfloat16):
    factor_of = shard_levels(rng, extent, pieces, -0.22, 0.18) if pieces else 1.0
    array = jax.random.normal(rng, extent, jnp.float32) * scale * factor_of
    return jnp.minimum(jnp.maximum(array, -most), most).astype(kind)


def bell_draw_with(key, shape, spread, reach, cuts, heavy, kind=jnp.bfloat16):
    array = spread * jax.random.normal(key, shape, jnp.float32)
    if cuts:
        array = array * shard_levels(key, shape, cuts, -0.22, 0.18)
    return jnp.clip(raised(array, jax.random.fold_in(key, 3), *heavy), -reach, reach).astype(kind)


def setup_inputs(seed: int = 0) -> dict:
    seeds = jax.random.split(jax.random.key(seed), 6)
    gate_pre = bell_draw_with(seeds[0], (TOKENS, FF), 1.0, 16.0, ((0, 12), (1, 64)), (1, 0, 64, 4.0))
    up_pre = scatter_about(seeds[1], (TOKENS, FF), 1.0, 6.0, ((0, 12), (1, 64)))
    down_weight = scatter_about(seeds[2], (FF, D), FF ** -0.5, 0.0390625, ((0, 64), (1, 12)))
    out_grad = scatter_about(seeds[3], (TOKENS, D), 1.0, 6.0, ((0, 64), (1, 12)))
    noised = draw_noised(jax.random.fold_in(seeds[5], 71), 0)
    return {"gate_pre": gate_pre, "up_pre": up_pre, "down_weight": down_weight, "out_grad": out_grad, "noised": noised}


def reference(gate_pre, up_pre, down_weight, out_grad, noised):
    gate = gate_pre.astype(jnp.float32)
    upper = up_pre.astype(jnp.float32)
    sigma = jax.nn.sigmoid(gate)
    silu_gate = gate * sigma
    hidden = (silu_gate * upper).astype(jnp.bfloat16)
    layer_out = jnp.dot(hidden, down_weight, preferred_element_type=jnp.float32).astype(jnp.bfloat16)
    flags = noised.astype(jnp.float32)
    count = jnp.sum(flags)
    scaled = (out_grad.astype(jnp.float32) * flags[:, None] * (TOKENS / count)).astype(jnp.bfloat16)
    width = D // N_ROW
    hidden_grad = jnp.zeros((TOKENS, FF), jnp.float32)
    for block in range(N_ROW):
        part_scaled = scaled[:, block * width:(block + 1) * width]
        part_weight = down_weight[:, block * width:(block + 1) * width]
        term = jnp.dot(part_scaled, part_weight.T, preferred_element_type=jnp.float32)
        hidden_grad = hidden_grad + term.astype(jnp.bfloat16).astype(jnp.float32)
    slope = sigma * (1.0 + gate * (1.0 - sigma))
    gate_grad = (hidden_grad * upper * slope).astype(jnp.bfloat16)
    up_grad = (hidden_grad * silu_gate).astype(jnp.bfloat16)
    weight_grad = jnp.dot(hidden.T, scaled, preferred_element_type=jnp.float32).astype(jnp.bfloat16)
    return (layer_out, gate_grad, up_grad, weight_grad)
```

```python
import jax
import jax.numpy as jnp
from jax import lax
from jax.experimental import pallas as pl
from jax.experimental.pallas import tpu as pltpu
from jax.sharding import PartitionSpec as P

MESH = pl.DeviceIdType.MESH
F32 = jnp.float32
BF16 = jnp.bfloat16
NZ, NX, NY, NL = 3, 4, 8, 4
COPIES = 128


def kernel(
    gate_ref, up_ref, w_ref, og_ref, noised_ref,
    lo_ref, gg_ref, ug_ref, wg_ref,
    x0_send, x0_recv, s_buf, ht, h_buf, cl_send, cl_recv, cy_own, cy_recv,
    po, ps, pr, y_send, y_recv, l_send, l_recv, fin, fin_recv,
    gt, x_send, x_recv, z_send, z_recv,
    send_sem, recv_sem,
):
    tok, ff = gate_ref.shape
    own_tok, feat = og_ref.shape
    half = feat // 2
    pair = 2 * own_tok
    group = NL * pair
    tokens = tok * NZ * NX

    row, col = lax.axis_index("row"), lax.axis_index("col")
    zh, x = row // NX, row % NX
    c, chip = col % 2, col // 2
    y, zl = chip // NL, chip % NL
    first = c == 0
    sgn = 1 - 2 * c

    def at(zh_=zh, x_=x, y_=y, zl_=zl, c_=c):
        return (zh_ * NX + x_, (y_ * NL + zl_) * 2 + c_)

    def xi(d):
        return (x + sgn * d + 2 * NX) % NX

    def yi(d):
        return (y + sgn * d + 2 * NY) % NY

    sibling = at(c_=1 - c)
    x_long, x_short = at(x_=xi(1)), at(x_=xi(-1))
    y_long, y_short = at(y_=yi(1)), at(y_=yi(-1))
    zl_at = [at(zl_=(zl + k) % NL) for k in range(NL)]
    zh_at = [at(zh_=(zh + k) % NZ) for k in range(NZ)]

    started = []

    def send(src, dst, device):
        i = len(started)
        copy = pltpu.make_async_remote_copy(
            src_ref=src, dst_ref=dst, send_sem=send_sem.at[i], recv_sem=recv_sem.at[i],
            device_id=device, device_id_type=MESH,
        )
        copy.start()
        started.append(copy)
        return copy

    barrier = pltpu.get_barrier_semaphore()
    partners = [sibling, x_long, x_short, y_long, y_short] + zl_at[1:] + zh_at[1:]
    for partner in partners:
        pl.semaphore_signal(barrier, inc=1, device_id=partner, device_id_type=MESH)

    flags_row = noised_ref[...].astype(F32)
    i0 = lax.broadcasted_iota(jnp.int32, (own_tok, own_tok), 0)
    i1 = lax.broadcasted_iota(jnp.int32, (own_tok, own_tok), 1)
    flags = jnp.sum(
        jnp.where(i0 == i1, jnp.broadcast_to(flags_row, (own_tok, own_tok)), 0.0),
        axis=1, keepdims=True,
    )
    masked = og_ref[...].astype(F32) * flags
    own_count = jnp.sum(jnp.broadcast_to(flags_row, (8, own_tok)), axis=1, keepdims=True)
    lo, hi = masked[:, :half], masked[:, half:]
    x0_send[0:own_tok, :] = jnp.where(first, hi, lo)
    x0_send[own_tok:own_tok + 8, :] = jnp.broadcast_to(own_count, (8, half))
    kept = jnp.where(first, lo, hi)

    pl.semaphore_wait(barrier, len(partners))
    x0 = send(x0_send, x0_recv, sibling)

    def parts():
        gate = gate_ref[...].astype(F32)
        sigma = jax.nn.sigmoid(gate)
        return gate, up_ref[...].astype(F32), sigma, gate * sigma

    _, upper, _, silu = parts()
    ht[row] = jnp.transpose((silu * upper)).astype(BF16)

    hb = ff // 2
    halves = [pl.ds(0, hb), pl.ds(hb, hb)]
    z_cp = [[send(ht.at[row, p], ht.at[row, p], zh_at[k]) for k in (1, 2)] for p in halves]

    def block(k, d):
        return ((zh - k + NZ) % NZ) * NX + xi(d)

    def x_start(k, p):
        b = ht.at[block(k, 0), p]
        return [send(b, b, x_long), send(b, b, x_short)]

    def x_forward(cps, k, p):
        cps[0].wait_recv()
        b = ht.at[block(k, -1), p]
        cps.append(send(b, b, x_long))

    whole = pl.ds(0, ff)
    xa = x_start(0, whole)

    x0.wait_recv()
    got = x0_recv[0:own_tok, :]
    cols = pl.ds(pl.multiple_of(c * half, 128), half)

    def s_block(y_, l_, n=1):
        return s_buf.at[pl.ds(pl.multiple_of((y_ * NL + l_) * pair, 16), n * pair), cols]

    s_block(y, zl)[...] = jnp.concatenate(
        [jnp.where(first, kept, got), jnp.where(first, got, kept)], axis=0
    ).astype(BF16)
    cl_send[...] = own_count + x0_recv[own_tok:own_tok + 8, 0:128]
    own = s_block(y, zl)
    l_cp = [send(own, own, zl_at[k]) for k in range(1, NL)]
    cl_cp = [send(cl_send, cl_recv.at[k - 1], zl_at[k]) for k in range(1, NL)]

    y_cp = {}

    def y_start(k, way, step):
        sign = 1 if way == 0 else -1
        b = s_block(yi(-sign * step), (zl - k + NL) % NL)
        if step:
            y_cp[k, way, step - 1].wait_recv()
        y_cp[k, way, step] = send(b, b, (y_long, y_short)[way])

    y_start(0, 0, 0)
    y_start(0, 1, 0)
    for k in range(1, NL):
        l_cp[k - 1].wait_recv()
        y_start(k, 0, 0)
        y_start(k, 1, 0)
    sib_cp = {}

    def to_sibling(d):
        b = s_block(yi(d), 0, NL)
        sib_cp[d % NY] = send(b, b, sibling)

    to_sibling(0)
    total = cl_send[...]
    for k in range(1, NL):
        cl_cp[k - 1].wait_recv()
        total = total + cl_recv[k - 1]
    cy_own[...] = total
    cy_cp = {}

    def cy_start(way, step):
        if step:
            cy_cp[way, step - 1].wait_recv()
        slot = way * 4 + step
        src = cy_recv.at[slot - 1] if step else cy_own
        cy_cp[way, step] = send(src, cy_recv.at[slot], (y_long, y_short)[way])

    cy_start(0, 0)
    cy_start(1, 0)

    x_forward(xa, 0, whole)
    for k in range(NL):
        y_start(k, 0, 1)
        y_start(k, 1, 1)
    cy_start(0, 1)
    cy_start(1, 1)
    to_sibling(-1)
    to_sibling(1)

    def to_rows(k, d):
        b = block(k, d)
        h_buf[pl.ds(pl.multiple_of(b * tok, tok), tok), :] = jnp.transpose(ht[b])

    to_rows(0, 0)

    xb = []
    for k in (1, 2):
        z_cp[0][k - 1].wait_recv()
        xb.append(x_start(k, halves[0]))
    for k in range(NL):
        y_start(k, 0, 2)
        y_start(k, 1, 2)
    cy_start(0, 2)
    cy_start(1, 2)
    to_sibling(-2)
    to_sibling(2)
    for k in (1, 2):
        x_forward(xb[k - 1], k, halves[0])
    xa[1].wait_recv()
    to_rows(0, -1)
    to_rows(0, 1)
    xc = []
    for k in (1, 2):
        z_cp[1][k - 1].wait_recv()
        xc.append(x_start(k, halves[1]))
    for k in range(NL):
        y_start(k, 0, 3)
    cy_start(0, 3)
    xa[2].wait_recv()
    to_rows(0, 2)
    for k in range(NL):
        y_cp[k, 1, 2].wait_recv()
    to_sibling(-3)
    to_sibling(3)
    for k in (1, 2):
        x_forward(xc[k - 1], k, halves[1])
    to_rows(1, 0)
    to_rows(2, 0)
    for k in range(NL):
        y_cp[k, 0, 3].wait_recv()
    to_sibling(4)
    for k in (1, 2):
        xb[k - 1][1].wait_recv()
        xc[k - 1][1].wait_recv()
        to_rows(k, 1)
        to_rows(k, -1)

    for d in range(NY):
        sib_cp[d].wait_recv()

    span = NX * tok
    pieces = {"A0": (1, 0, hb), "B0": (2, 0, hb), "A1": (1, hb, hb), "B1": (2, hb, hb), "C": (0, 0, ff)}
    g_cp = {}

    def g_product(name):
        k, r0, n = pieces[name]
        other = (zh + k) % NZ
        rows = s_buf[pl.ds(pl.multiple_of(other * span, span), span), :]
        out = lax.dot_general(
            w_ref[r0:r0 + n, :], rows, (((1,), (1,)), ((), ())), preferred_element_type=F32
        )
        for x_ in range(NX):
            d = (sgn * (x_ - x) + 2 * NX) % NX
            gt[k, d, r0:r0 + n, :] = out[:, x_ * tok:(x_ + 1) * tok]

    def g_send(name, slot, value, device):
        k, r0, n = pieces[name]
        x_send[slot, k, r0:r0 + n, :] = value.astype(BF16)
        g_cp[name, slot] = send(
            x_send.at[slot, k, pl.ds(r0, n)], x_recv.at[slot, k, pl.ds(r0, n)], device
        )

    def g_got(name, slot):
        k, r0, n = pieces[name]
        g_cp[name, slot].wait_recv()
        return x_recv[slot, k, r0:r0 + n, :].astype(F32)

    def g_own(name, d):
        k, r0, n = pieces[name]
        return gt[k, d, r0:r0 + n, :]

    def g_first(name):
        g_product(name)
        g_send(name, 0, g_own(name, 2), x_long)
        g_send(name, 1, g_own(name, 3), x_short)

    def g_second(name):
        g_send(name, 2, g_own(name, 1) + g_got(name, 0), x_long)

    zr_cp = {}

    def g_last(name):
        k, r0, n = pieces[name]
        value = g_own(name, 0) + g_got(name, 1) + g_got(name, 2)
        if k == 0:
            return value
        z_send[k - 1, r0:r0 + n, :] = value.astype(BF16)
        zr_cp[name] = send(
            z_send.at[k - 1, pl.ds(r0, n)], z_recv.at[k - 1, pl.ds(r0, n)], zh_at[k]
        )
        return None

    p_cp = {}

    def p_product(d):
        d = d % NY
        out = jnp.dot(
            h_buf[pl.ds(pl.multiple_of(yi(d) * group, 16), group), :], w_ref[...],
            preferred_element_type=F32,
        )
        mine = jnp.where(first, out[:, :half], out[:, half:])
        theirs = jnp.where(first, out[:, half:], out[:, :half]).astype(BF16)
        for a in range(NL):
            slot = (a - zl - 1 + 2 * NL) % NL
            po[d, slot] = mine[a * pair:(a + 1) * pair]
            ps[d, slot] = theirs[a * pair:(a + 1) * pair]
        p_cp[d] = send(ps.at[d], pr.at[(NY - d) % NY], sibling)

    def p_wait(d):
        p_cp[(NY - d) % NY].wait_recv()

    ry_cp = {}

    def p_sum(d, g):
        d = d % NY
        return po[d, 2 * g:2 * g + 2] + pr[d, 2 * g:2 * g + 2].astype(F32)

    def ry_send(way, step, g):
        d = 4 - step if way == 0 else step - 3
        slot = way * 4 + step
        value = p_sum(d, g)
        if step:
            ry_cp[way, step - 1, g].wait_recv()
            value = value + y_recv[slot - 1, 2 * g:2 * g + 2].astype(F32)
        y_send[slot, 2 * g:2 * g + 2] = value.astype(BF16)
        ry_cp[way, step, g] = send(
            y_send.at[slot, pl.ds(2 * g, 2)], y_recv.at[slot, pl.ds(2 * g, 2)],
            (y_long, y_short)[way],
        )

    def ry_last(g):
        ry_cp[0, 3, g].wait_recv()
        ry_cp[1, 2, g].wait_recv()
        return (
            p_sum(0, g) + y_recv[3, 2 * g:2 * g + 2].astype(F32)
            + y_recv[6, 2 * g:2 * g + 2].astype(F32)
        )

    g_first("A0")
    g_first("B0")
    for k in (1, 2):
        xb[k - 1][2].wait_recv()
        xc[k - 1][2].wait_recv()
        to_rows(k, 2)
    p_product(4)
    p_product(3)
    p_product(-3)
    g_first("A1")
    g_first("B1")
    p_wait(4)
    for g in range(2):
        ry_send(0, 0, g)
    p_wait(5)
    for g in range(2):
        ry_send(1, 0, g)
    p_product(2)
    p_product(-2)
    g_second("A0")
    g_second("B0")
    p_product(1)
    p_product(-1)
    g_first("C")
    p_product(0)
    g_second("A1")
    g_second("B1")
    p_wait(3)
    p_wait(6)
    for g in range(2):
        ry_send(0, 1, g)
        ry_send(1, 1, g)
    g_last("A0")
    g_last("B0")
    for d in (2, 7):
        p_wait(d)
    for g in range(2):
        ry_send(0, 2, g)
        ry_send(1, 2, g)
    g_last("A1")
    g_last("B1")
    g_second("C")

    for way in range(2):
        cy_cp[way, 3 - way].wait_recv()
    count = cy_own[...]
    for slot in range(7):
        count = count + cy_recv[slot]
    scale = tokens / count

    nb = 256
    scale_w = jnp.broadcast_to(scale[0:1, 0:1], (1, nb))

    def w_product(j):
        acc = jnp.zeros((ff, nb), F32)
        for i in range(NZ * NX // 2):
            acc = acc + jnp.dot(
                jnp.concatenate([ht[2 * i], ht[2 * i + 1]], axis=1),
                s_buf[2 * tok * i:2 * tok * (i + 1), j * nb:(j + 1) * nb],
                preferred_element_type=F32,
            )
        wg_ref[:, j * nb:(j + 1) * nb] = (acc * scale_w).astype(BF16)

    w_product(0)
    for d in (1, 0):
        p_wait(d)
    for g in range(2):
        ry_send(0, 3, g)
    w_product(1)
    w_product(2)
    tail = g_last("C")
    fl_cp = []
    v0 = ry_last(0)
    for j in range(2):
        l_send[j] = v0[j].astype(BF16)
        fl_cp.append(send(l_send.at[j], l_recv.at[j], zl_at[j + 1]))
    v1 = ry_last(1)
    l_send[2] = v1[0].astype(BF16)
    fl_cp.append(send(l_send.at[2], l_recv.at[2], zl_at[3]))
    out = v1[1]
    for j in range(3):
        fl_cp[j].wait_recv()
        out = out + l_recv[j].astype(F32)
    fin[0] = out[:own_tok]
    fin[1] = out[own_tok:]
    fin_cp = send(fin.at[1 - c], fin_recv, sibling)

    for cp in zr_cp.values():
        cp.wait_recv()
    grad = jnp.transpose(tail + z_recv[0].astype(F32) + z_recv[1].astype(F32))
    grad = grad * jnp.broadcast_to(scale[0:1, 0:1], (1, ff))
    gate, upper, sigma, silu = parts()
    gg_ref[...] = (grad * upper * (sigma * (1.0 + gate * (1.0 - sigma)))).astype(BF16)
    ug_ref[...] = (grad * silu).astype(BF16)

    fin_cp.wait_recv()
    mine, theirs = fin[c], fin_recv[...]
    lo_ref[:, :half] = jnp.where(first, mine, theirs).astype(BF16)
    lo_ref[:, half:] = jnp.where(first, theirs, mine).astype(BF16)
    for copy in started:
        copy.wait_send()


def body(gate_pre, up_pre, down_weight, out_grad, noised):
    tok, ff = gate_pre.shape
    own, feat = out_grad.shape
    half, pair, tokens = feat // 2, 2 * own, tok * NZ * NX
    vmem = pl.BlockSpec(memory_space=pltpu.VMEM)
    return pl.pallas_call(
        kernel,
        out_shape=(
            jax.ShapeDtypeStruct((own, feat), BF16),
            jax.ShapeDtypeStruct((tok, ff), BF16),
            jax.ShapeDtypeStruct((tok, ff), BF16),
            jax.ShapeDtypeStruct((ff, feat), BF16),
        ),
        in_specs=[vmem] * 5,
        out_specs=(vmem,) * 4,
        scratch_shapes=[
            pltpu.VMEM((own + 8, half), F32),
            pltpu.VMEM((own + 8, half), F32),
            pltpu.VMEM((tokens, feat), BF16),
            pltpu.VMEM((NZ * NX, ff, tok), BF16),
            pltpu.VMEM((tokens, ff), BF16),
            pltpu.VMEM((8, 128), F32),
            pltpu.VMEM((NL - 1, 8, 128), F32),
            pltpu.VMEM((8, 128), F32),
            pltpu.VMEM((NY - 1, 8, 128), F32),
            pltpu.VMEM((NY, NL, pair, half), F32),
            pltpu.VMEM((NY, NL, pair, half), BF16),
            pltpu.VMEM((NY, NL, pair, half), BF16),
            pltpu.VMEM((NY - 1, NL, pair, half), BF16),
            pltpu.VMEM((NY - 1, NL, pair, half), BF16),
            pltpu.VMEM((NL - 1, pair, half), BF16),
            pltpu.VMEM((NL - 1, pair, half), BF16),
            pltpu.VMEM((2, own, half), F32),
            pltpu.VMEM((own, half), F32),
            pltpu.VMEM((NZ, NX, ff, tok), F32),
            pltpu.VMEM((NX - 1, NZ, ff, tok), BF16),
            pltpu.VMEM((NX - 1, NZ, ff, tok), BF16),
            pltpu.VMEM((NZ - 1, ff, tok), BF16),
            pltpu.VMEM((NZ - 1, ff, tok), BF16),
            pltpu.SemaphoreType.DMA((COPIES,)),
            pltpu.SemaphoreType.DMA((COPIES,)),
        ],
        compiler_params=pltpu.CompilerParams(
            collective_id=0, has_side_effects=True, vmem_limit_bytes=56 * 1024 * 1024
        ),
        cost_estimate=pl.CostEstimate(
            flops=6 * tokens * ff * feat, bytes_accessed=4 * ff * feat, transcendentals=tok * ff
        ),
    )(gate_pre, up_pre, down_weight, out_grad, noised.reshape(1, own))


def solution(mesh):
    return jax.shard_map(
        body,
        mesh=mesh,
        in_specs=(P("row", "col"), P("row", "col"), P("col", "row"), P("col", "row"), P("col")),
        out_specs=(P("col", "row"), P("row", "col"), P("row", "col"), P("col", "row")),
        check_vma=False,
    )
```

```python
import jax
import jax.numpy as jnp
from jax import lax
from jax.experimental import pallas as pl
from jax.experimental.pallas import tpu as pltpu
from jax.sharding import PartitionSpec as P

MESH = pl.DeviceIdType.MESH
F32 = jnp.float32
BF16 = jnp.bfloat16
NZ, NX, NY, NL = 3, 4, 8, 4
COPIES = 200


def kernel(
    gate_hbm, up_hbm, w_hbm, og_hbm, noised_hbm,
    lo_ref, gg_ref, ug_ref, wg_ref,
    gate_ref, up_ref, w_ref, og_ref, noised_ref,
    x0_send, x0_recv, s_buf, ht, cl_send, cl_recv, cy_own, cy_recv,
    po, ps, pr, y_send, y_recv, l_send, l_recv,
    x_send, x_recv, z_send, z_recv,
    in_sem, zl_sem, fin_sem, send_sem, recv_sem,
):
    ff, tok = gate_ref.shape
    own_tok, feat = og_ref.shape
    half = feat // 2
    pair = 2 * own_tok
    tokens = tok * NZ * NX

    loads = [
        pltpu.make_async_copy(src, dst, in_sem.at[i])
        for i, (src, dst) in enumerate([
            (og_hbm, og_ref), (noised_hbm, noised_ref), (gate_hbm, gate_ref),
            (up_hbm, up_ref), (w_hbm, w_ref),
        ])
    ]
    for load in loads:
        load.start()

    row, col = lax.axis_index("row"), lax.axis_index("col")
    zh, x = row // NX, row % NX
    c, chip = col % 2, col // 2
    y, zl = chip // NL, chip % NL
    first = c == 0
    sgn = 1 - 2 * c

    def at(zh_=zh, x_=x, y_=y, zl_=zl, c_=c):
        return (zh_ * NX + x_, (y_ * NL + zl_) * 2 + c_)

    def xi(d):
        return (x + sgn * d + 2 * NX) % NX

    def yi(d):
        return (y + sgn * d + 2 * NY) % NY

    sibling = at(c_=1 - c)
    x_at = [at(x_=xi(d)) for d in range(NX)]
    y_way = (at(y_=yi(1)), at(y_=yi(-1)))
    zl_at = [at(zl_=(zl + k) % NL) for k in range(NL)]
    zh_at = [at(zh_=(zh + k) % NZ) for k in range(NZ)]

    started = []

    def send(src, dst, device, arrived=None):
        i = len(started)
        copy = pltpu.make_async_remote_copy(
            src_ref=src, dst_ref=dst, send_sem=send_sem.at[i],
            recv_sem=recv_sem.at[i] if arrived is None else arrived,
            device_id=device, device_id_type=MESH,
        )
        copy.start()
        started.append(copy)
        return copy

    barrier = pltpu.get_barrier_semaphore()
    partners = [sibling, *y_way] + x_at[1:] + zl_at[1:] + zh_at[1:]
    partners += [at(zl_=(zl + k) % NL, c_=1 - c) for k in range(1, NL)]
    for partner in partners:
        pl.semaphore_signal(barrier, inc=1, device_id=partner, device_id_type=MESH)

    loads[0].wait()
    loads[1].wait()
    flags_row = noised_ref[...].astype(F32)
    i0 = lax.broadcasted_iota(jnp.int32, (own_tok, own_tok), 0)
    i1 = lax.broadcasted_iota(jnp.int32, (own_tok, own_tok), 1)
    flags = jnp.sum(
        jnp.where(i0 == i1, jnp.broadcast_to(flags_row, (own_tok, own_tok)), 0.0),
        axis=1, keepdims=True,
    )
    masked = og_ref[...].astype(F32) * flags
    own_count = jnp.sum(jnp.broadcast_to(flags_row, (8, own_tok)), axis=1, keepdims=True)
    lo, hi = masked[:, :half], masked[:, half:]
    x0_send[0:own_tok, :] = jnp.where(first, hi, lo)
    x0_send[own_tok:own_tok + 8, :] = jnp.broadcast_to(own_count, (8, half))

    loads[2].wait()
    loads[3].wait()

    def parts():
        gate = gate_ref[...].astype(F32)
        sigma = jax.nn.sigmoid(gate)
        return gate, up_ref[...].astype(F32), sigma, gate * sigma

    _, upper, _, silu = parts()
    ht[row] = (silu * upper).astype(BF16)

    up = zl // 2

    def near(j):
        rising = (j - 1) + 1 - (zl + 3 - (j - 1)) // 4
        falling = 3 - ((j - 1) + 1 - (3 - zl + 3 - (j - 1)) // 4)
        return (1 - up) * rising + up * falling

    cuts, r0 = [], 0
    for n in (112, 112, 112, 80):
        cuts.append((r0, n))
        r0 += n

    def block(k, d):
        return ((zh - k + NZ) % NZ) * NX + xi(d)

    pl.semaphore_wait(barrier, len(partners))
    x0 = send(x0_send, x0_recv, sibling)
    z_cp = []

    def z_start(q):
        b = ht.at[row, pl.ds(*cuts[q])]
        z_cp.append([send(b, b, zh_at[k]) for k in (1, 2)])

    z_start(0)

    x_cp = {}

    def x_spread(k, q, a, n):
        b = ht.at[block(k, 0), pl.ds(a, n)]
        for d in (2, 1, 3):
            x_cp[k, q, d] = send(b, b, x_at[d])

    x_spread(0, 0, 0, ff)

    def z_arrive(q):
        for k in (1, 2):
            z_cp[q][k - 1].wait_recv()
            x_spread(k, q, *cuts[q])

    def x_arrive(k, d):
        for q in range(len(cuts) if k else 1):
            x_cp[k, q, d].wait_recv()

    x0.wait_recv()
    got = x0_recv[0:own_tok, :]
    cols = pl.ds(pl.multiple_of(c * half, 128), half)

    def s_block(y_, l_, n=1):
        return s_buf.at[pl.ds(pl.multiple_of((y_ * NL + l_) * pair, 16), n * pair), cols]

    kept = jnp.where(first, og_ref[:, :half].astype(F32), og_ref[:, half:].astype(F32)) * flags
    s_block(y, zl)[...] = jnp.concatenate(
        [jnp.where(first, kept, got), jnp.where(first, got, kept)], axis=0
    ).astype(BF16)
    cl_send[...] = own_count + x0_recv[own_tok:own_tok + 8, 0:128]
    own = s_block(y, zl)
    l_cp = [send(own, own, zl_at[k], zl_sem.at[zl]) for k in range(1, NL)]

    def zl_arrive(j):
        b = s_block(y, near(j))
        pltpu.make_async_remote_copy(
            src_ref=b, dst_ref=b, send_sem=send_sem.at[0], recv_sem=zl_sem.at[near(j)],
            device_id=sibling, device_id_type=MESH,
        ).wait_recv()

    def of_chip(j):
        return near(j) if j else zl

    y_cp = {}

    def y_start(k, way, step):
        sign = 1 if way == 0 else -1
        b = s_block(yi(-sign * step), of_chip(k))
        if step:
            y_cp[k, way, step - 1].wait_recv()
        y_cp[k, way, step] = send(b, b, y_way[way])

    sib_cp = {}

    def to_sibling(d):
        b = s_block(yi(d), 0, NL)
        sib_cp[d % NY] = send(b, b, sibling)

    def chunk_to_sibling(k, d):
        b = s_block(yi(d), of_chip(k))
        sib_cp[d % NY, k] = send(b, b, sibling)

    cy_cp = {}

    def cy_start(way, step):
        if step:
            cy_cp[way, step - 1].wait_recv()
        slot = way * 4 + step
        src = cy_recv.at[slot - 1] if step else cy_own
        cy_cp[way, step] = send(src, cy_recv.at[slot], y_way[way])

    y_start(0, 0, 0)
    y_start(0, 1, 0)
    cl_cp = [send(cl_send, cl_recv.at[k - 1], zl_at[k]) for k in range(1, NL)]
    for q in range(1, len(cuts)):
        z_start(q)

    p_cp = {}

    def p_block(k, d):
        b = block(k, d)
        rows = pl.ds(pl.multiple_of(b * tok, tok), tok)
        out = jnp.dot(jnp.transpose(ht[b]), w_ref[...], preferred_element_type=F32)
        po[rows, :] = jnp.where(first, out[:, :half], out[:, half:])
        ps[rows, :] = jnp.where(first, out[:, half:], out[:, :half]).astype(BF16)
        p_cp[k, d] = send(ps.at[rows], pr.at[rows], sibling)

    loads[4].wait()
    p_block(0, 0)
    y_start(0, 0, 1)
    y_start(0, 1, 1)
    for k in range(1, NL):
        zl_arrive(k)
        y_start(k, 0, 0)
        y_start(k, 1, 0)
    z_arrive(0)
    to_sibling(0)
    total = cl_send[...]
    for k in range(1, NL):
        cl_cp[k - 1].wait_recv()
        total = total + cl_recv[k - 1]
    cy_own[...] = total
    cy_start(0, 0)
    cy_start(1, 0)
    y_start(0, 0, 2)
    y_start(0, 1, 2)
    z_arrive(1)
    for k in range(1, NL):
        y_start(k, 0, 1)
        y_start(k, 1, 1)
    to_sibling(-1)
    to_sibling(1)
    y_start(0, 0, 3)
    cy_start(0, 1)
    cy_start(1, 1)
    for d in (1, 3, 2):
        x_arrive(0, d)
        p_block(0, NX - d)
    z_arrive(2)
    for k in range(1, NL):
        y_start(k, 0, 2)
        y_start(k, 1, 2)
    to_sibling(-2)
    to_sibling(2)
    cy_start(0, 2)
    cy_start(1, 2)
    z_arrive(3)
    p_block(1, 0)
    p_block(2, 0)
    for k in range(NL):
        if k:
            y_start(k, 0, 3)
        y_cp[k, 1, 2].wait_recv()
        chunk_to_sibling(k, -3)
        chunk_to_sibling(k, 3)
    cy_start(0, 3)

    span = NX * tok
    pieces = {(k, q): cut for k in (1, 2) for q, cut in enumerate(cuts)}
    pieces[0, 0] = (0, ff)
    g_cp = {}

    def g_start(k, q):
        a, n = pieces[k, q]
        rows = s_buf[pl.ds(pl.multiple_of((zh + k) % NZ * span, span), span), :]
        out = lax.dot_general(
            w_ref[a:a + n, :], rows, (((1,), (1,)), ((), ())), preferred_element_type=F32
        ).astype(BF16)
        for x_ in range(NX):
            d = (sgn * (x_ - x) + 2 * NX) % NX
            x_send[d, k, a:a + n, :] = out[:, x_ * tok:(x_ + 1) * tok]
        for d in (2, 1, 3):
            g_cp[k, q, d] = send(
                x_send.at[d, k, pl.ds(a, n)], x_recv.at[d - 1, k, pl.ds(a, n)], x_at[d]
            )

    zr_cp = []

    def g_sum(k, q):
        a, n = pieces[k, q]
        value = x_send[0, k, a:a + n, :].astype(F32)
        for d in (1, 3, 2):
            g_cp[k, q, d].wait_recv()
            value = value + x_recv[d - 1, k, a:a + n, :].astype(F32)
        return value

    def g_last(q):
        for k in (1, 2):
            a, n = pieces[k, q]
            z_send[k - 1, a:a + n, :] = g_sum(k, q).astype(BF16)
            zr_cp.append(send(
                z_send.at[k - 1, pl.ds(a, n)], z_recv.at[k - 1, pl.ds(a, n)], zh_at[k]
            ))

    ry_cp = {}

    def p_sum(d, j):
        to = near(3 - j) if j < NL - 1 else zl
        rows = pl.ds(pl.multiple_of((yi(d) * NL + to) * pair, 16), pair)
        return po[rows, :] + pr[rows, :].astype(F32)

    def ry_send(way, step, j):
        d = 4 - step if way == 0 else step - 3
        slot = way * 4 + step
        value = p_sum(d, j)
        if step:
            ry_cp[way, step - 1, j].wait_recv()
            value = value + y_recv[slot - 1, j].astype(F32)
        y_send[slot, j] = value.astype(BF16)
        ry_cp[way, step, j] = send(y_send.at[slot, j], y_recv.at[slot, j], y_way[way])

    def ry_both(step):
        for j in range(NL):
            ry_send(0, step, j)
            if step < 3:
                ry_send(1, step, j)

    for d in (1, 3, 2):
        for k in (1, 2):
            x_arrive(k, d)
            p_block(k, NX - d)
    for k in range(NL):
        y_cp[k, 0, 3].wait_recv()
        chunk_to_sibling(k, 4)
    for copy in p_cp.values():
        copy.wait_recv()
    ry_both(0)
    for copy in sib_cp.values():
        copy.wait_recv()
    for q in range(len(cuts)):
        g_start(1, q)
        g_start(2, q)
    ry_both(1)
    g_start(0, 0)

    for way in range(2):
        cy_cp[way, 3 - way].wait_recv()
    count = cy_own[...]
    for slot in range(7):
        count = count + cy_recv[slot]
    scale = tokens / count

    nb = 256
    scale_w = jnp.broadcast_to(scale[0:1, 0:1], (1, nb))

    def w_product(j):
        acc = jnp.zeros((ff, nb), F32)
        for i in range(NZ * NX // 2):
            acc = acc + jnp.dot(
                jnp.concatenate([ht[2 * i], ht[2 * i + 1]], axis=1),
                s_buf[2 * tok * i:2 * tok * (i + 1), j * nb:(j + 1) * nb],
                preferred_element_type=F32,
            )
        wg_ref[:, j * nb:(j + 1) * nb] = (acc * scale_w).astype(BF16)

    g_last(0)
    ry_both(2)
    w_product(0)
    g_last(1)
    ry_both(3)
    g_last(2)
    w_product(1)

    def piece(c_):
        return pl.ds(pl.multiple_of(16 * c_, 16), 32)

    def last_slot(zl_, c_):
        return l_recv.at[zl_ * 2 + c_], fin_sem.at[zl_ * 2 + c_]

    for j in range(NL):
        ry_cp[0, 3, j].wait_recv()
        ry_cp[1, 2, j].wait_recv()
        out = p_sum(0, j) + y_recv[3, j].astype(F32) + y_recv[6, j].astype(F32)
        l_send[j] = out.astype(BF16)
        dst, arrived = last_slot(zl, c)
        if j < NL - 1:
            for c_ in range(2):
                send(l_send.at[j, pl.ds(16 * c_, 32)], dst, at(zl_=near(3 - j), c_=c_), arrived)
        else:
            send(l_send.at[j, piece(1 - c)], dst, sibling, arrived)
    g_last(3)
    tail = g_sum(0, 0)
    w_product(2)

    def arrived_piece(zl_, c_):
        dst, arrived = last_slot(zl_, c_)
        pltpu.make_async_remote_copy(
            src_ref=dst, dst_ref=dst, send_sem=send_sem.at[0], recv_sem=arrived,
            device_id=sibling, device_id_type=MESH,
        ).wait_recv()
        return l_recv[zl_ * 2 + c_].astype(F32)

    mine = jnp.where(first, out[0:32], out[16:48])
    theirs = arrived_piece(zl, 1 - c)
    for j in range(1, NL):
        mine = mine + arrived_piece(near(j), c)
        theirs = theirs + arrived_piece(near(j), 1 - c)
    mine = jnp.where(first, mine[0:own_tok], mine[8:8 + own_tok])
    theirs = jnp.where(first, theirs[0:own_tok], theirs[8:8 + own_tok])
    lo_ref[:, :half] = jnp.where(first, mine, theirs).astype(BF16)
    lo_ref[:, half:] = jnp.where(first, theirs, mine).astype(BF16)

    for copy in zr_cp:
        copy.wait_recv()
    grad = (tail + z_recv[0].astype(F32) + z_recv[1].astype(F32)) * scale[0:1, :]
    gate, upper, sigma, silu = parts()
    gg_ref[...] = (grad * upper * (sigma * (1.0 + gate * (1.0 - sigma)))).astype(BF16)
    ug_ref[...] = (grad * silu).astype(BF16)

    for copy in started:
        copy.wait_send()


def write_kernel(*refs):
    n = len(refs) // 2
    sems = refs[-1]
    copies = [pltpu.make_async_copy(refs[i], refs[n + i], sems.at[i]) for i in range(n)]
    for copy in copies:
        copy.start()
    for copy in copies:
        copy.wait()


def written(arrays):
    return pl.pallas_call(
        write_kernel,
        out_shape=tuple(jax.ShapeDtypeStruct(a.shape, a.dtype) for a in arrays),
        in_specs=[pl.BlockSpec(memory_space=pltpu.VMEM)] * len(arrays),
        out_specs=(pl.BlockSpec(memory_space=pl.ANY),) * len(arrays),
        scratch_shapes=[pltpu.SemaphoreType.DMA((len(arrays),))],
        compiler_params=pltpu.CompilerParams(vmem_limit_bytes=4 * 1024 * 1024),
    )(*arrays)


def body(gate_pre, up_pre, down_weight, out_grad, noised):
    tok, ff = gate_pre.shape
    own, feat = out_grad.shape
    half, pair, tokens = feat // 2, 2 * own, tok * NZ * NX
    vmem = pl.BlockSpec(memory_space=pltpu.VMEM)
    layer_out, gate_grad, up_grad, weight_grad = written(pl.pallas_call(
        kernel,
        out_shape=(
            pltpu.VMEM((own, feat), BF16),
            pltpu.VMEM((ff, tok), BF16),
            pltpu.VMEM((ff, tok), BF16),
            pltpu.VMEM((ff, feat), BF16),
        ),
        in_specs=[pl.BlockSpec(memory_space=pl.ANY)] * 5,
        out_specs=(vmem,) * 4,
        scratch_shapes=[
            pltpu.VMEM((ff, tok), BF16),
            pltpu.VMEM((ff, tok), BF16),
            pltpu.VMEM((ff, feat), BF16),
            pltpu.VMEM((own, feat), BF16),
            pltpu.VMEM((1, own), jnp.int32),
            pltpu.VMEM((own + 8, half), F32),
            pltpu.VMEM((own + 8, half), F32),
            pltpu.VMEM((tokens, feat), BF16),
            pltpu.VMEM((NZ * NX, ff, tok), BF16),
            pltpu.VMEM((8, 128), F32),
            pltpu.VMEM((NL - 1, 8, 128), F32),
            pltpu.VMEM((8, 128), F32),
            pltpu.VMEM((NY - 1, 8, 128), F32),
            pltpu.VMEM((tokens, half), F32),
            pltpu.VMEM((tokens, half), BF16),
            pltpu.VMEM((tokens, half), BF16),
            pltpu.VMEM((NY - 1, NL, pair, half), BF16),
            pltpu.VMEM((NY - 1, NL, pair, half), BF16),
            pltpu.VMEM((NL, pair, half), BF16),
            pltpu.VMEM((2 * NL, 32, half), BF16),
            pltpu.VMEM((NX, NZ, ff, tok), BF16),
            pltpu.VMEM((NX - 1, NZ, ff, tok), BF16),
            pltpu.VMEM((NZ - 1, ff, tok), BF16),
            pltpu.VMEM((NZ - 1, ff, tok), BF16),
            pltpu.SemaphoreType.DMA((5,)),
            pltpu.SemaphoreType.DMA((NL,)),
            pltpu.SemaphoreType.DMA((2 * NL,)),
            pltpu.SemaphoreType.DMA((COPIES,)),
            pltpu.SemaphoreType.DMA((COPIES,)),
        ],
        compiler_params=pltpu.CompilerParams(
            collective_id=0, has_side_effects=True, vmem_limit_bytes=56 * 1024 * 1024
        ),
        cost_estimate=pl.CostEstimate(
            flops=6 * tokens * ff * feat, bytes_accessed=4 * ff * feat, transcendentals=tok * ff
        ),
    )(gate_pre.T, up_pre.T, down_weight, out_grad, noised.reshape(1, own)))
    return layer_out, gate_grad.T, up_grad.T, weight_grad


def solution(mesh):
    return jax.shard_map(
        body,
        mesh=mesh,
        in_specs=(P("row", "col"), P("row", "col"), P("col", "row"), P("col", "row"), P("col")),
        out_specs=(P("col", "row"), P("row", "col"), P("row", "col"), P("col", "row")),
        check_vma=False,
    )
```

```python
import jax
import jax.numpy as jnp
from jax import lax
from jax.experimental import pallas as pl
from jax.experimental.pallas import tpu as pltpu
from jax.sharding import PartitionSpec as P

MESH = pl.DeviceIdType.MESH
F32 = jnp.float32
BF16 = jnp.bfloat16
NZ, NX, NY, NL = 3, 4, 8, 4
COPIES = 200


def kernel(
    gate_hbm, up_hbm, w_hbm, og_hbm, noised_hbm,
    lo_ref, gg_ref, ug_ref, wg_ref,
    gate_ref, up_ref, w_ref, og_ref, noised_ref,
    x0_send, x0_recv, s_buf, ht, cl_send, cl_recv, cy_own, cy_recv,
    po, ps, pr, y_send, y_recv, l_send, l_recv,
    x_send, x_recv, x_pass, z_send, z_recv,
    in_sem, zl_sem, fin_sem, send_sem, recv_sem,
):
    ff, tok = gate_ref.shape
    own_tok, feat = og_ref.shape
    half = feat // 2
    pair = 2 * own_tok
    tokens = tok * NZ * NX

    loads = [
        pltpu.make_async_copy(src, dst, in_sem.at[i])
        for i, (src, dst) in enumerate([
            (og_hbm, og_ref), (noised_hbm, noised_ref), (gate_hbm, gate_ref),
            (up_hbm, up_ref), (w_hbm, w_ref),
        ])
    ]
    for load in loads:
        load.start()

    row, col = lax.axis_index("row"), lax.axis_index("col")
    zh, x = row // NX, row % NX
    c, chip = col % 2, col // 2
    y, zl = chip // NL, chip % NL
    first = c == 0
    sgn = 1 - 2 * c

    def at(zh_=zh, x_=x, y_=y, zl_=zl, c_=c):
        return (zh_ * NX + x_, (y_ * NL + zl_) * 2 + c_)

    def xi(d):
        return (x + sgn * d + 2 * NX) % NX

    def yi(d):
        return (y + sgn * d + 2 * NY) % NY

    sibling = at(c_=1 - c)
    x_at = [at(x_=xi(d)) for d in range(NX)]
    y_way = (at(y_=yi(1)), at(y_=yi(-1)))
    zl_at = [at(zl_=(zl + k) % NL) for k in range(NL)]
    zh_at = [at(zh_=(zh + k) % NZ) for k in range(NZ)]

    started = []

    def send(src, dst, device, arrived=None):
        i = len(started)
        copy = pltpu.make_async_remote_copy(
            src_ref=src, dst_ref=dst, send_sem=send_sem.at[i],
            recv_sem=recv_sem.at[i] if arrived is None else arrived,
            device_id=device, device_id_type=MESH,
        )
        copy.start()
        started.append(copy)
        return copy

    barrier = pltpu.get_barrier_semaphore()
    partners = [sibling, *y_way] + x_at[1:] + zl_at[1:] + zh_at[1:]
    partners += [at(zl_=(zl + k) % NL, c_=1 - c) for k in range(1, NL)]
    for partner in partners:
        pl.semaphore_signal(barrier, inc=1, device_id=partner, device_id_type=MESH)

    loads[0].wait()
    loads[1].wait()
    flags_row = noised_ref[...].astype(F32)
    i0 = lax.broadcasted_iota(jnp.int32, (own_tok, own_tok), 0)
    i1 = lax.broadcasted_iota(jnp.int32, (own_tok, own_tok), 1)
    flags = jnp.sum(
        jnp.where(i0 == i1, jnp.broadcast_to(flags_row, (own_tok, own_tok)), 0.0),
        axis=1, keepdims=True,
    )
    masked = og_ref[...].astype(F32) * flags
    own_count = jnp.sum(jnp.broadcast_to(flags_row, (8, own_tok)), axis=1, keepdims=True)
    lo, hi = masked[:, :half], masked[:, half:]
    x0_send[0:own_tok, :] = jnp.where(first, hi, lo)
    x0_send[own_tok:own_tok + 8, :] = jnp.broadcast_to(own_count, (8, half))

    loads[2].wait()
    loads[3].wait()

    def parts():
        gate = gate_ref[...].astype(F32)
        sigma = jax.nn.sigmoid(gate)
        return gate, up_ref[...].astype(F32), sigma, gate * sigma

    _, upper, _, silu = parts()
    ht[row] = (silu * upper).astype(BF16)

    up = zl // 2

    def near(j):
        rising = (j - 1) + 1 - (zl + 3 - (j - 1)) // 4
        falling = 3 - ((j - 1) + 1 - (3 - zl + 3 - (j - 1)) // 4)
        return (1 - up) * rising + up * falling

    cuts, r0 = [], 0
    for n in (112, 112, 112, 80):
        cuts.append((r0, n))
        r0 += n

    def block(k, d):
        return ((zh - k + NZ) % NZ) * NX + xi(d)

    pl.semaphore_wait(barrier, len(partners))
    x0 = send(x0_send, x0_recv, sibling)
    z_cp = []

    def z_start(q):
        b = ht.at[row, pl.ds(*cuts[q])]
        z_cp.append([send(b, b, zh_at[k]) for k in (1, 2)])

    z_start(0)

    x_cp = {}

    def x_spread(k, q, a, n):
        b = ht.at[block(k, 0), pl.ds(a, n)]
        for d in (2, 1, 3):
            x_cp[k, q, d] = send(b, b, x_at[d])

    x_spread(0, 0, 0, ff)

    def z_arrive(q):
        for k in (1, 2):
            z_cp[q][k - 1].wait_recv()
            x_spread(k, q, *cuts[q])

    def x_arrive(k, d):
        for q in range(len(cuts) if k else 1):
            x_cp[k, q, d].wait_recv()

    x0.wait_recv()
    got = x0_recv[0:own_tok, :]
    cols = pl.ds(pl.multiple_of(c * half, 128), half)

    def s_block(y_, l_, n=1):
        return s_buf.at[pl.ds(pl.multiple_of((y_ * NL + l_) * pair, 16), n * pair), cols]

    kept = jnp.where(first, og_ref[:, :half].astype(F32), og_ref[:, half:].astype(F32)) * flags
    s_block(y, zl)[...] = jnp.concatenate(
        [jnp.where(first, kept, got), jnp.where(first, got, kept)], axis=0
    ).astype(BF16)
    cl_send[...] = own_count + x0_recv[own_tok:own_tok + 8, 0:128]
    own = s_block(y, zl)
    l_cp = [send(own, own, zl_at[k], zl_sem.at[zl]) for k in range(1, NL)]

    def zl_arrive(j):
        b = s_block(y, near(j))
        pltpu.make_async_remote_copy(
            src_ref=b, dst_ref=b, send_sem=send_sem.at[0], recv_sem=zl_sem.at[near(j)],
            device_id=sibling, device_id_type=MESH,
        ).wait_recv()

    def of_chip(j):
        return near(j) if j else zl

    y_cp = {}

    def y_start(k, way, step):
        sign = 1 if way == 0 else -1
        b = s_block(yi(-sign * step), of_chip(k))
        if step:
            y_cp[k, way, step - 1].wait_recv()
        y_cp[k, way, step] = send(b, b, y_way[way])

    sib_cp = {}

    def to_sibling(d):
        b = s_block(yi(d), 0, NL)
        sib_cp[d % NY] = send(b, b, sibling)

    def chunk_to_sibling(k, d):
        b = s_block(yi(d), of_chip(k))
        sib_cp[d % NY, k] = send(b, b, sibling)

    cy_cp = {}

    def cy_start(way, step):
        if step:
            cy_cp[way, step - 1].wait_recv()
        slot = way * 4 + step
        src = cy_recv.at[slot - 1] if step else cy_own
        cy_cp[way, step] = send(src, cy_recv.at[slot], y_way[way])

    y_start(0, 0, 0)
    y_start(0, 1, 0)
    cl_cp = [send(cl_send, cl_recv.at[k - 1], zl_at[k]) for k in range(1, NL)]

    p_cp = {}

    def p_block(k, d):
        b = block(k, d)
        rows = pl.ds(pl.multiple_of(b * tok, tok), tok)
        out = jnp.dot(jnp.transpose(ht[b]), w_ref[...], preferred_element_type=F32)
        po[rows, :] = jnp.where(first, out[:, :half], out[:, half:])
        ps[rows, :] = jnp.where(first, out[:, half:], out[:, :half]).astype(BF16)
        p_cp[k, d] = send(ps.at[rows], pr.at[rows], sibling)

    loads[4].wait()
    p_block(0, 0)
    y_start(0, 0, 1)
    y_start(0, 1, 1)
    for k in range(1, NL):
        zl_arrive(k)
        if k == NL - 1:
            for q in range(1, len(cuts)):
                z_start(q)
        y_start(k, 0, 0)
        y_start(k, 1, 0)
    z_arrive(0)
    to_sibling(0)
    total = cl_send[...]
    for k in range(1, NL):
        cl_cp[k - 1].wait_recv()
        total = total + cl_recv[k - 1]
    cy_own[...] = total
    cy_start(0, 0)
    cy_start(1, 0)
    y_start(0, 0, 2)
    y_start(0, 1, 2)
    z_arrive(1)
    for k in range(1, NL):
        y_start(k, 0, 1)
        y_start(k, 1, 1)
    to_sibling(-1)
    to_sibling(1)
    y_start(0, 0, 3)
    cy_start(0, 1)
    cy_start(1, 1)
    for d in (1, 3, 2):
        x_arrive(0, d)
        p_block(0, NX - d)
    z_arrive(2)
    for k in range(1, NL):
        y_start(k, 0, 2)
        y_start(k, 1, 2)
    to_sibling(-2)
    to_sibling(2)
    cy_start(0, 2)
    cy_start(1, 2)
    z_arrive(3)
    p_block(1, 0)
    p_block(2, 0)
    for k in range(NL):
        if k:
            y_start(k, 0, 3)
        y_cp[k, 1, 2].wait_recv()
        chunk_to_sibling(k, -3)
        chunk_to_sibling(k, 3)
    cy_start(0, 3)

    span = NX * tok
    pieces = {(k, q): cut for k in (1, 2) for q, cut in enumerate(cuts)}
    pieces[0, 0] = (0, ff)
    g_cp = {}

    def g_start(k, q):
        a, n = pieces[k, q]
        rows = s_buf[pl.ds(pl.multiple_of((zh + k) % NZ * span, span), span), :]
        out = lax.dot_general(
            w_ref[a:a + n, :], rows, (((1,), (1,)), ((), ())), preferred_element_type=F32
        ).astype(BF16)
        for x_ in range(NX):
            d = (sgn * (x_ - x) + 2 * NX) % NX
            x_send[d, k, a:a + n, :] = out[:, x_ * tok:(x_ + 1) * tok]
        for slot, d, way in ((0, 2, 1), (2, 3, 3)):
            g_cp[k, q, slot] = send(
                x_send.at[d, k, pl.ds(a, n)], x_recv.at[slot, k, pl.ds(a, n)], x_at[way]
            )

    def g_pass(k, q):
        a, n = pieces[k, q]
        g_cp[k, q, 0].wait_recv()
        value = x_send[1, k, a:a + n, :].astype(F32) + x_recv[0, k, a:a + n, :].astype(F32)
        x_pass[k, a:a + n, :] = value.astype(BF16)
        g_cp[k, q, 1] = send(
            x_pass.at[k, pl.ds(a, n)], x_recv.at[1, k, pl.ds(a, n)], x_at[1]
        )

    def g_both(q):
        g_pass(1, q)
        g_pass(2, q)

    zr_cp = []

    def g_sum(k, q):
        a, n = pieces[k, q]
        value = x_send[0, k, a:a + n, :].astype(F32)
        for slot in (2, 1):
            g_cp[k, q, slot].wait_recv()
            value = value + x_recv[slot, k, a:a + n, :].astype(F32)
        return value

    def g_last(q):
        for k in (1, 2):
            a, n = pieces[k, q]
            z_send[k - 1, a:a + n, :] = g_sum(k, q).astype(BF16)
            zr_cp.append(send(
                z_send.at[k - 1, pl.ds(a, n)], z_recv.at[k - 1, pl.ds(a, n)], zh_at[k]
            ))

    ry_cp = {}

    def p_sum(d, j):
        to = near(3 - j) if j < NL - 1 else zl
        rows = pl.ds(pl.multiple_of((yi(d) * NL + to) * pair, 16), pair)
        return po[rows, :] + pr[rows, :].astype(F32)

    def ry_send(way, step, j):
        d = 4 - step if way == 0 else step - 3
        slot = way * 4 + step
        value = p_sum(d, j)
        if step:
            ry_cp[way, step - 1, j].wait_recv()
            value = value + y_recv[slot - 1, j].astype(F32)
        y_send[slot, j] = value.astype(BF16)
        ry_cp[way, step, j] = send(y_send.at[slot, j], y_recv.at[slot, j], y_way[way])

    def ry_both(step):
        for j in range(NL):
            ry_send(0, step, j)
            if step < 3:
                ry_send(1, step, j)

    for d in (1, 3, 2):
        for k in (1, 2):
            x_arrive(k, d)
            p_block(k, NX - d)
    for k in range(NL):
        y_cp[k, 0, 3].wait_recv()
        chunk_to_sibling(k, 4)
    for copy in p_cp.values():
        copy.wait_recv()
    ry_both(0)
    for copy in sib_cp.values():
        copy.wait_recv()
    for q in range(len(cuts)):
        g_start(1, q)
        g_start(2, q)
    ry_both(1)
    g_both(0)
    g_both(1)
    g_start(0, 0)
    g_last(0)
    g_both(2)
    g_last(1)

    for way in range(2):
        cy_cp[way, 3 - way].wait_recv()
    count = cy_own[...]
    for slot in range(7):
        count = count + cy_recv[slot]
    scale = tokens / count

    nb = 256
    scale_w = jnp.broadcast_to(scale[0:1, 0:1], (1, nb))

    def w_product(j):
        acc = jnp.zeros((ff, nb), F32)
        for i in range(NZ * NX // 2):
            acc = acc + jnp.dot(
                jnp.concatenate([ht[2 * i], ht[2 * i + 1]], axis=1),
                s_buf[2 * tok * i:2 * tok * (i + 1), j * nb:(j + 1) * nb],
                preferred_element_type=F32,
            )
        wg_ref[:, j * nb:(j + 1) * nb] = (acc * scale_w).astype(BF16)

    ry_both(2)
    g_both(3)
    g_last(2)
    w_product(0)
    ry_both(3)
    g_last(3)

    def piece(c_):
        return pl.ds(pl.multiple_of(16 * c_, 16), 32)

    def last_slot(zl_, c_):
        return l_recv.at[zl_ * 2 + c_], fin_sem.at[zl_ * 2 + c_]

    for j in range(NL):
        ry_cp[0, 3, j].wait_recv()
        ry_cp[1, 2, j].wait_recv()
        out = p_sum(0, j) + y_recv[3, j].astype(F32) + y_recv[6, j].astype(F32)
        l_send[j] = out.astype(BF16)
        dst, arrived = last_slot(zl, c)
        if j < NL - 1:
            for c_ in range(2):
                send(l_send.at[j, pl.ds(16 * c_, 32)], dst, at(zl_=near(3 - j), c_=c_), arrived)
        else:
            send(l_send.at[j, piece(1 - c)], dst, sibling, arrived)
    g_pass(0, 0)
    w_product(1)
    tail = g_sum(0, 0)
    w_product(2)

    def arrived_piece(zl_, c_):
        dst, arrived = last_slot(zl_, c_)
        pltpu.make_async_remote_copy(
            src_ref=dst, dst_ref=dst, send_sem=send_sem.at[0], recv_sem=arrived,
            device_id=sibling, device_id_type=MESH,
        ).wait_recv()
        return l_recv[zl_ * 2 + c_].astype(F32)

    mine = jnp.where(first, out[0:32], out[16:48])
    theirs = arrived_piece(zl, 1 - c)
    for j in range(1, NL):
        mine = mine + arrived_piece(near(j), c)
        theirs = theirs + arrived_piece(near(j), 1 - c)
    mine = jnp.where(first, mine[0:own_tok], mine[8:8 + own_tok])
    theirs = jnp.where(first, theirs[0:own_tok], theirs[8:8 + own_tok])
    lo_ref[:, :half] = jnp.where(first, mine, theirs).astype(BF16)
    lo_ref[:, half:] = jnp.where(first, theirs, mine).astype(BF16)

    for copy in zr_cp:
        copy.wait_recv()
    grad = (tail + z_recv[0].astype(F32) + z_recv[1].astype(F32)) * scale[0:1, :]
    gate, upper, sigma, silu = parts()
    gg_ref[...] = (grad * upper * (sigma * (1.0 + gate * (1.0 - sigma)))).astype(BF16)
    ug_ref[...] = (grad * silu).astype(BF16)

    for copy in started:
        copy.wait_send()


def write_kernel(*refs):
    n = len(refs) // 2
    sems = refs[-1]
    copies = [pltpu.make_async_copy(refs[i], refs[n + i], sems.at[i]) for i in range(n)]
    for copy in copies:
        copy.start()
    for copy in copies:
        copy.wait()


def written(arrays):
    return pl.pallas_call(
        write_kernel,
        out_shape=tuple(jax.ShapeDtypeStruct(a.shape, a.dtype) for a in arrays),
        in_specs=[pl.BlockSpec(memory_space=pltpu.VMEM)] * len(arrays),
        out_specs=(pl.BlockSpec(memory_space=pl.ANY),) * len(arrays),
        scratch_shapes=[pltpu.SemaphoreType.DMA((len(arrays),))],
        compiler_params=pltpu.CompilerParams(vmem_limit_bytes=4 * 1024 * 1024),
    )(*arrays)


def body(gate_pre, up_pre, down_weight, out_grad, noised):
    tok, ff = gate_pre.shape
    own, feat = out_grad.shape
    half, pair, tokens = feat // 2, 2 * own, tok * NZ * NX
    vmem = pl.BlockSpec(memory_space=pltpu.VMEM)
    layer_out, gate_grad, up_grad, weight_grad = written(pl.pallas_call(
        kernel,
        out_shape=(
            pltpu.VMEM((own, feat), BF16),
            pltpu.VMEM((ff, tok), BF16),
            pltpu.VMEM((ff, tok), BF16),
            pltpu.VMEM((ff, feat), BF16),
        ),
        in_specs=[pl.BlockSpec(memory_space=pl.ANY)] * 5,
        out_specs=(vmem,) * 4,
        scratch_shapes=[
            pltpu.VMEM((ff, tok), BF16),
            pltpu.VMEM((ff, tok), BF16),
            pltpu.VMEM((ff, feat), BF16),
            pltpu.VMEM((own, feat), BF16),
            pltpu.VMEM((1, own), jnp.int32),
            pltpu.VMEM((own + 8, half), F32),
            pltpu.VMEM((own + 8, half), F32),
            pltpu.VMEM((tokens, feat), BF16),
            pltpu.VMEM((NZ * NX, ff, tok), BF16),
            pltpu.VMEM((8, 128), F32),
            pltpu.VMEM((NL - 1, 8, 128), F32),
            pltpu.VMEM((8, 128), F32),
            pltpu.VMEM((NY - 1, 8, 128), F32),
            pltpu.VMEM((tokens, half), F32),
            pltpu.VMEM((tokens, half), BF16),
            pltpu.VMEM((tokens, half), BF16),
            pltpu.VMEM((NY - 1, NL, pair, half), BF16),
            pltpu.VMEM((NY - 1, NL, pair, half), BF16),
            pltpu.VMEM((NL, pair, half), BF16),
            pltpu.VMEM((2 * NL, 32, half), BF16),
            pltpu.VMEM((NX, NZ, ff, tok), BF16),
            pltpu.VMEM((NX - 1, NZ, ff, tok), BF16),
            pltpu.VMEM((NZ, ff, tok), BF16),
            pltpu.VMEM((NZ - 1, ff, tok), BF16),
            pltpu.VMEM((NZ - 1, ff, tok), BF16),
            pltpu.SemaphoreType.DMA((5,)),
            pltpu.SemaphoreType.DMA((NL,)),
            pltpu.SemaphoreType.DMA((2 * NL,)),
            pltpu.SemaphoreType.DMA((COPIES,)),
            pltpu.SemaphoreType.DMA((COPIES,)),
        ],
        compiler_params=pltpu.CompilerParams(
            collective_id=0, has_side_effects=True, vmem_limit_bytes=56 * 1024 * 1024
        ),
        cost_estimate=pl.CostEstimate(
            flops=6 * tokens * ff * feat, bytes_accessed=4 * ff * feat, transcendentals=tok * ff
        ),
    )(gate_pre.T, up_pre.T, down_weight, out_grad, noised.reshape(1, own)))
    return layer_out, gate_grad.T, up_grad.T, weight_grad


def solution(mesh):
    return jax.shard_map(
        body,
        mesh=mesh,
        in_specs=(P("row", "col"), P("row", "col"), P("col", "row"), P("col", "row"), P("col")),
        out_specs=(P("col", "row"), P("row", "col"), P("row", "col"), P("col", "row")),
        check_vma=False,
    )
```
